256 devices in a mesh: gx: 16 (over z, y_lo), gy: 16 (over y_hi, x, core).
Axes of the slice: x: 4, y: 4 (y_hi: 2, y_lo: 2; y = y_hi * 2 + y_lo), z: 8, core: 2. Of those that a mesh axis runs over, the one named last changes fastest.
Arguments:
- fields: float32 [6, 4096, 4096], P(None, 'gx', 'gy'), may hold values from -6 to 6
- inv_eps: float32 [4096, 4096], P('gx', 'gy'), may hold values from 0.75 to 1
- fwd_dft: float32 [3, 2, 3, 4096, 4096], P(None, None, None, 'gx', 'gy'), may hold values from -6 to 6
- phase_start: float32 [3], replicated, may hold values from -3.140625 to 3.140625
- omega: float32 [3], replicated, may hold values from 0.3 to 1.2
- mask: int32 [4096, 4096], P('gx', 'gy'), may hold values 0 or 1
Outputs:
- fields_out: float32 [6, 4096, 4096], P(None, 'gx', 'gy')
- gradient: float32 [4096, 4096], P('gx', 'gy')
The draws below stay inside these ranges and needn't reach their ends.
All inputs are finite; a program needn't handle non-finite values. No bound on the sum of `mask` on one device may be relied on, other than what follows from the above.
Results may differ from the reference program's by a relative error of at most 0.000034.
Values sent between devices are 32-bit elements; how exact they have to be, the bound alone decides.
No kernel may reach another device: no remote copies, remote signals or barrier semaphores. Data moves between devices by JAX's collectives and lax.ppermute only.
A program may use at most 128 MiB of HBM per device.

```python
import math
import jax
import jax.numpy as jnp
import numpy as np
from jax import lax

STEPS = 24
NF = 3
RADIUS = 3
NX = 4096
NY = 4096


def place_ends(array, rng, least, high):
    place = [jax.random.randint(jax.random.fold_in(rng, axis), (), 0, length) for axis, length in enumerate(array.shape)]
    widest = array.shape.index(max(array.shape))
    next_to = place[:widest] + [(place[widest] + 1) % array.shape[widest]] + place[widest + 1:]
    return array.at[tuple(place)].set(least).at[tuple(next_to)].set(high)


def levels(stream_key, shape, pieces, smallest, high):
    def one(dim, parts):
        heights = jax.random.uniform(jax.random.fold_in(jax.random.fold_in(stream_key, 6), dim), (parts,), jnp.float32, smallest / len(pieces), high / len(pieces))
        return jnp.repeat(jnp.exp(heights), shape[dim] // parts).reshape((-1,) + (1,) * (len(shape) - dim - 1))

    level = one(*pieces[0])
    for cut in pieces[1:]:
        level = level * one(*cut)
    return level


def noise(rng, extent, deviation, bound, shards=(), kind=jnp.bfloat16):
    result = deviation * jax.random.normal(rng, extent, jnp.float32)
    if shards:
        result = result * levels(rng, extent, shards, -0.22, 0.18)
    return jnp.clip(result, -bound, bound).astype(kind)


def setup_inputs(seed: int = 0) -> dict:
    splits = jax.random.split(jax.random.key(seed), 7)
    fields = noise(splits[0], (6, NX, NY), 1.0, 6.0, ((1, 16), (2, 16)), jnp.float32)
    inv_eps = jnp.clip(0.75 + 0.25 * jax.random.uniform(splits[1], (NX, NY), jnp.float32) ** levels(splits[1], (NX, NY), ((0, 16), (1, 16)), -0.2, 0.2), 0.75, 1.0)
    fwd_dft = noise(splits[2], (NF, 2, 3, NX, NY), 1.0, 6.0, ((3, 16), (4, 16)), jnp.float32)
    phase_start = jnp.clip(jax.random.uniform(splits[3], (NF,), jnp.float32, -3.140625, 3.140625), -3.140625, 3.140625)
    omega = jnp.clip(jnp.exp(jax.random.uniform(splits[4], (NF,), jnp.float32, math.log(0.3), math.log(1.2))), 0.3, 1.2)
    mask = place_ends((jax.random.randint(splits[5], (NX, NY), 0, 4) < 3).astype(jnp.int32), jax.random.fold_in(splits[5], 1), 0, 1)
    return {"fields": fields, "inv_eps": inv_eps, "fwd_dft": fwd_dft, "phase_start": phase_start, "omega": omega, "mask": mask}


courant = 0.68

def filter_table(radius):
    offsets = np.arange(-radius, radius + 1)
    dist = np.sqrt(offsets[:, None] ** 2 + offsets[None, :] ** 2)
    table = np.maximum(0.0, radius - dist)
    return table / table.sum()

def update_h(ex, ey, ez, hx, hy, hz, ey_nx, ez_nx, ex_ny, ez_ny):
    hx = hx - courant * (ez_ny - ez)
    hy = hy + courant * (ez_nx - ez)
    hz = hz - courant * (ey_nx - ey - (ex_ny - ex))
    return (hx, hy, hz)

def update_e(ex, ey, ez, hx, hy, hz, inv_eps, hy_px, hz_px, hx_py, hz_py):
    factor = courant * inv_eps
    ex = ex + factor * (hz - hz_py)
    ey = ey - factor * (hz - hz_px)
    ez = ez + factor * (hy - hy_px - (hx - hx_py))
    return (ex, ey, ez)

def accumulate(acc, efield, count, phase_start, omega):
    theta = phase_start + omega * count.astype(jnp.float32)
    coefs = jnp.stack([jnp.cos(theta), jnp.sin(theta)], axis=1) / STEPS
    return acc + coefs[:, :, None, None, None] * efield[None, None]

def reference(fields, inv_eps, fwd_dft, phase_start, omega, mask):
    acc = jnp.zeros((NF, 2, 3) + fields.shape[1:], jnp.float32)

    def advance(count, carry):
        state, acc = carry
        ex, ey, ez, hx, hy, hz = [state[k] for k in range(6)]
        hx, hy, hz = update_h(ex, ey, ez, hx, hy, hz, jnp.roll(ey, -1, 0), jnp.roll(ez, -1, 0), jnp.roll(ex, -1, 1), jnp.roll(ez, -1, 1))
        ex, ey, ez = update_e(ex, ey, ez, hx, hy, hz, inv_eps, jnp.roll(hy, 1, 0), jnp.roll(hz, 1, 0), jnp.roll(hx, 1, 1), jnp.roll(hz, 1, 1))
        acc = accumulate(acc, jnp.stack([ex, ey, ez]), count, phase_start, omega)
        return (jnp.stack([ex, ey, ez, hx, hy, hz]), acc)
    state, acc = lax.fori_loop(0, STEPS, advance, (fields, acc))
    prod = acc[:, 0] * fwd_dft[:, 0] - acc[:, 1] * fwd_dft[:, 1]
    raw = lax.optimization_barrier(jnp.sum(prod, axis=(0, 1))) * mask.astype(jnp.float32)
    table = filter_table(RADIUS)
    gradient = jnp.zeros_like(raw)
    for ia in range(2 * RADIUS + 1):
        for ib in range(2 * RADIUS + 1):
            weight = float(table[ia, ib])
            if weight > 0.0:
                shifted = jnp.roll(jnp.roll(raw, RADIUS - ia, 0), RADIUS - ib, 1)
                gradient = gradient + weight * shifted
    return (state, gradient)
```

```python
import functools

import jax
import jax.numpy as jnp
import numpy as np
from jax import lax
from jax.experimental import pallas as pl
from jax.experimental.pallas import tpu as pltpu
from jax.sharding import PartitionSpec as P

STEPS = 24
NF = 3
RADIUS = 3
COURANT = 0.68

T = 256
PAD = 32
ROWS = T + 2 * PAD
CHUNK = 39
FIRST = (ROWS - 8 * CHUNK) // 2
LANES = 128
DEEP = STEPS + 2
PLANES = 6 * NF
K = 8 * 2 * NF

f32 = jnp.float32
bf16 = jnp.bfloat16


def filter_table():
    offsets = np.arange(-RADIUS, RADIUS + 1)
    dist = np.sqrt(offsets[:, None] ** 2 + offsets[None, :] ** 2)
    table = np.maximum(0.0, RADIUS - dist)
    return table / table.sum()


def lane_iota():
    return lax.broadcasted_iota(jnp.int32, (8, LANES), 1)


def turn(x, shift, axis):
    size = x.shape[axis]
    shift = shift % size
    return x if shift == 0 else pltpu.roll(x, shift, axis)


def left_slot(group):
    return 32 * ((group + 1) % 4)


def pack_kernel(fields, inv_eps, fwd, mask, xs0, xs1, ys0, ys1, f7, fw, mk, xbuf, ybuf, sems):
    px = lax.rem(lax.axis_index("gx"), 2)
    py = lax.rem(lax.axis_index("gy"), 2)
    loads = [
        pltpu.make_async_copy(fields, f7.at[pl.ds(0, 6)], sems.at[0]),
        pltpu.make_async_copy(inv_eps, f7.at[6], sems.at[1]),
        pltpu.make_async_copy(mask, mk, sems.at[2]),
        pltpu.make_async_copy(fwd, fw.at[pl.ds(0, PLANES)], sems.at[3]),
    ]
    for copy in loads:
        copy.start()
    for copy in loads:
        copy.wait()
    fw[PLANES] = mk[...].astype(f32)

    sub = lax.broadcasted_iota(jnp.int32, (8, T), 0)
    for k in range(7):
        extra = [m for m in range(3 * k, 3 * k + 3) if m <= PLANES]
        xbuf[0, k, pl.ds(8, 24)] = f7[k, pl.ds(T - 24, 24)]
        xbuf[1, k, pl.ds(0, 24)] = f7[k, pl.ds(0, 24)]
        low, high = f7[k, pl.ds(T - 32, 8)], f7[k, pl.ds(24, 8)]
        for jj, m in enumerate(extra):
            low = jnp.where(sub // 2 == jj, turn(fw[m, pl.ds(T - 8, 8)], 2 * jj + 2, 0), low)
            high = jnp.where(sub // 2 == jj + 1, turn(fw[m, pl.ds(0, 8)], 2 * jj + 2, 0), high)
        xbuf[0, k, pl.ds(0, 8)] = low
        xbuf[1, k, pl.ds(24, 8)] = high

    lane = lane_iota()

    def rows(j, _):
        for k in range(7):
            extra = [m for m in range(3 * k, 3 * k + 3) if m <= PLANES]
            last = first = jnp.zeros((8, LANES), f32)
            for g in range(4):
                at = pl.ds(pl.multiple_of(64 * g + 8 * j, 8), 8)
                a = f7[k, at, pl.ds(0, LANES)]
                b = f7[k, at, pl.ds(LANES, LANES)]
                for jj, m in enumerate(extra):
                    fa = fw[m, at, pl.ds(0, LANES)]
                    fb = fw[m, at, pl.ds(LANES, LANES)]
                    a = jnp.where(lane // 2 == 13 + jj, turn(fa, 26 + 2 * jj, 1), a)
                    b = jnp.where(lane // 2 == 48 + jj, turn(fb, 98 + 2 * jj, 1), b)
                first = jnp.where(lane // 32 == g, turn(a, 32 * g, 1), first)
                last = jnp.where(lane // 32 == (g + 1) % 4, turn(b, left_slot(g) - 96, 1), last)
            to = pl.ds(pl.multiple_of(8 * j, 8), 8)
            ybuf[0, k, to] = last
            ybuf[1, k, to] = first
        return 0

    lax.fori_loop(0, 8, rows, 0)
    stores = [
        pltpu.make_async_copy(xbuf.at[px], xs0, sems.at[0]),
        pltpu.make_async_copy(xbuf.at[1 - px], xs1, sems.at[1]),
        pltpu.make_async_copy(ybuf.at[py], ys0, sems.at[2]),
        pltpu.make_async_copy(ybuf.at[1 - py], ys1, sems.at[3]),
    ]
    for copy in stores:
        copy.start()
    for copy in stores:
        copy.wait()


def pack(fields, inv_eps, fwd, mask):
    any_space = pl.BlockSpec(memory_space=pl.ANY)
    x_slab = jax.ShapeDtypeStruct((7, 32, T), f32)
    y_slab = jax.ShapeDtypeStruct((7, 64, LANES), f32)
    return pl.pallas_call(
        pack_kernel,
        out_shape=(x_slab, x_slab, y_slab, y_slab),
        in_specs=[any_space] * 4,
        out_specs=(any_space,) * 4,
        scratch_shapes=[
            pltpu.VMEM((7, T, T), f32),
            pltpu.VMEM((PLANES + 1, T, T), f32),
            pltpu.VMEM((T, T), jnp.int32),
            pltpu.VMEM((2, 7, 32, T), f32),
            pltpu.VMEM((2, 7, 64, LANES), f32),
            pltpu.SemaphoreType.DMA((4,)),
        ],
        compiler_params=pltpu.CompilerParams(vmem_limit_bytes=24 * 2**20),
        name="pack",
    )(fields, inv_eps, fwd, mask)


def next_lane(tiles, lane):
    r = [turn(x, -1, 1) for x in tiles]
    return [jnp.where(lane == LANES - 1, r[(t + 1) % 3], r[t]) for t in range(3)]


def prev_lane(tiles, lane):
    r = [turn(x, 1, 1) for x in tiles]
    return [jnp.where(lane == 0, r[(t + 2) % 3], r[t]) for t in range(3)]


def main_kernel(coef, fields, inv_eps, fwd, mask, x0, x1, y0, y1, c0, c1, out, grad,
                stage, fst, mk, yl, yr, cl, ch, e, h, fac, raw, sems):
    px = lax.rem(lax.axis_index("gx"), 2)
    py = lax.rem(lax.axis_index("gy"), 2)
    own = pl.ds(PAD, T)
    copies, late = [], []
    for t in range(2):
        cols = pl.ds(LANES * t, LANES)
        copies.append(pltpu.make_async_copy(fields.at[:, :, cols], stage.at[pl.ds(0, 6), t, own], sems.at[t]))
        copies.append(pltpu.make_async_copy(inv_eps.at[:, cols], stage.at[6, t, own], sems.at[2 + t]))
        late.append(pltpu.make_async_copy(fwd.at[:, :, cols], fst.at[pl.ds(0, PLANES), t, own], sems.at[4 + t]))
    late.append(pltpu.make_async_copy(mask, mk, sems.at[6]))

    def edges(low, high, left, right, clow, chigh):
        res = []
        for t in range(2):
            cols = pl.ds(LANES * t, LANES)
            res.append(pltpu.make_async_copy(low.at[:, :, cols], stage.at[:, t, pl.ds(0, PAD)], sems.at[7 + t]))
            res.append(pltpu.make_async_copy(high.at[:, :, cols], stage.at[:, t, pl.ds(PAD + T, PAD)], sems.at[9 + t]))
        res.append(pltpu.make_async_copy(left, yl, sems.at[11]))
        res.append(pltpu.make_async_copy(right, yr, sems.at[12]))
        res.append(pltpu.make_async_copy(clow, cl, sems.at[13]))
        res.append(pltpu.make_async_copy(chigh, ch, sems.at[14]))
        return res

    for copy in copies:
        copy.start()
    for ix in range(2):
        for iy in range(2):
            @pl.when((px == ix) & (py == iy))
            def _():
                xs = (x1, x0) if ix == 0 else (x0, x1)
                ys = (y1, y0) if iy == 0 else (y0, y1)
                cs = (c1, c0) if ix == 0 else (c0, c1)
                for copy in edges(*xs, *ys, *cs):
                    copy.start()
    for copy in late:
        copy.start()
    for copy in copies:
        copy.wait()
    for copy in edges(x0, x1, y0, y1, c0, c1):
        copy.wait()

    lane = lane_iota()
    sub = lax.broadcasted_iota(jnp.int32, (8, LANES), 0)
    right_half = lane < 64

    def fill(j, _):
        at = pl.ds(pl.multiple_of(8 * j, 8), 8)
        for k in range(7):
            r, l = yr[k, at], yl[k, at]
            for g in range(4):
                to = pl.ds(pl.multiple_of(PAD + 64 * g + 8 * j, 8), 8)
                stage[k, 2, to] = jnp.where(right_half, turn(r, -32 * g, 1), turn(l, 96 - left_slot(g), 1))
                for jj, m in enumerate(range(3 * k, min(3 * k + 3, PLANES + 1))):
                    fst[m, 2, to] = jnp.where(
                        right_half, turn(r, -32 * g - 26 - 2 * jj, 1), turn(l, 126 - left_slot(g) - 2 * jj, 1)
                    )
        return 0

    lax.fori_loop(0, 8, fill, 0)
    zero = jnp.zeros((8, LANES), f32)
    for k in range(7):
        for j in range(4):
            a, b = cl[k, pl.ds(8 * j, 8)], ch[k, pl.ds(8 * j, 8)]
            stage[k, 2, pl.ds(8 * j, 8)] = jnp.where(right_half, turn(a, 32, 1), turn(a, 96, 1))
            stage[k, 2, pl.ds(PAD + T + 8 * j, 8)] = jnp.where(right_half, b, turn(b, 64, 1))
        a, b = cl[k, pl.ds(24, 8)], ch[k, pl.ds(0, 8)]
        for jj, m in enumerate(range(3 * k, min(3 * k + 3, PLANES + 1))):
            fst[m, 2, pl.ds(24, 8)] = jnp.where(right_half, turn(a, 32 - 26 - 2 * jj, 1), turn(a, 126 - 2 * jj, 1))
            fst[m, 2, pl.ds(PAD + T, 8)] = jnp.where(right_half, turn(b, -26 - 2 * jj, 1), turn(b, 94 - 2 * jj, 1))
            for t in range(2):
                lo, hi = stage[k, t, pl.ds(0, 8)], stage[k, t, pl.ds(ROWS - 8, 8)]
                fst[m, t, pl.ds(24, 8)] = jnp.where(sub >= 6, turn(lo, 6 - 2 * jj, 0), 0.0)
                fst[m, t, pl.ds(PAD + T, 8)] = jnp.where(sub < 2, turn(hi, -2 - 2 * jj, 0), 0.0)
            for t in range(3):
                for j in range(3):
                    fst[m, t, pl.ds(8 * j, 8)] = zero
                    fst[m, t, pl.ds(PAD + T + 8 + 8 * j, 8)] = zero

    def lift(v, _):
        at = pl.ds(FIRST + v, 8, stride=CHUNK)
        for t in range(3):
            for c in range(3):
                e[0, c, v, t] = stage[c, t, at, :]
                h[c, v, t] = stage[3 + c, t, at, :] * (1.0 / COURANT)
            fac[v, t] = stage[6, t, at, :] * (COURANT * COURANT)
        return 0

    lax.fori_loop(0, CHUNK, lift, 0)

    def step(n, _):
        def load_e(c, v):
            return [e[n, c, v, t] for t in range(3)]

        def load_h(c, v):
            return [h[c, v, t] for t in range(3)]

        def electric(v, ex, ey, ez, hx, hy, hz, hy_p, hz_p):
            hz_py, hx_py = prev_lane(hz, lane), prev_lane(hx, lane)
            for t in range(3):
                f = fac[v, t]
                e[n + 1, 0, v, t] = ex[t] + f * (hz[t] - hz_py[t])
                e[n + 1, 1, v, t] = ey[t] - f * (hz[t] - hz_p[t])
                e[n + 1, 2, v, t] = ez[t] + f * ((hy[t] - hy_p[t]) - (hx[t] - hx_py[t]))

        ey, ez = load_e(1, 0), load_e(2, 0)
        end = ([turn(x, -1, 0) for x in ey], [turn(x, -1, 0) for x in ez])
        hy_p = hz_p = None
        for v in range(CHUNK):
            ex = load_e(0, v)
            ey_n, ez_n = (load_e(1, v + 1), load_e(2, v + 1)) if v < CHUNK - 1 else end
            ex_ny, ez_ny = next_lane(ex, lane), next_lane(ez, lane)
            hx, hy, hz = load_h(0, v), load_h(1, v), load_h(2, v)
            for t in range(3):
                hx[t] = hx[t] - (ez_ny[t] - ez[t])
                hy[t] = hy[t] + (ez_n[t] - ez[t])
                hz[t] = hz[t] - ((ey_n[t] - ey[t]) - (ex_ny[t] - ex[t]))
                h[0, v, t], h[1, v, t], h[2, v, t] = hx[t], hy[t], hz[t]
            if v > 0:
                electric(v, ex, ey, ez, hx, hy, hz, hy_p, hz_p)
            ey, ez, hy_p, hz_p = ey_n, ez_n, hy, hz
        hy_p, hz_p = [turn(x, 1, 0) for x in hy_p], [turn(x, 1, 0) for x in hz_p]
        electric(0, load_e(0, 0), load_e(1, 0), load_e(2, 0), load_h(0, 0), load_h(1, 0), load_h(2, 0), hy_p, hz_p)
        return 0

    lax.fori_loop(0, STEPS, step, 0)

    for copy in late:
        copy.wait()
    for t in range(2):
        fst[PLANES, t, own] = mk[:, pl.ds(LANES * t, LANES)].astype(f32)

    def lower(v, _):
        at = pl.ds(FIRST + v, 8, stride=CHUNK)
        for t in range(2):
            for c in range(3):
                stage[c, t, at, :] = e[STEPS, c, v, t]
                stage[3 + c, t, at, :] = h[c, v, t] * COURANT
        return 0

    lax.fori_loop(0, CHUNK, lower, 0)
    stores = [
        pltpu.make_async_copy(stage.at[pl.ds(0, 6), t, own], out.at[:, :, pl.ds(LANES * t, LANES)], sems.at[t])
        for t in range(2)
    ]
    for copy in stores:
        copy.start()

    def gather(v, _):
        at = pl.ds(FIRST + v, 8, stride=CHUNK)
        total = [zero] * 3
        for c in range(3):
            w = jnp.concatenate(
                [jnp.concatenate([fst[3 * i + c, t, at, :] for t in range(3)], axis=1) for i in range(2 * NF)], axis=0
            )
            hi = w.astype(bf16)
            lo = (w - hi.astype(f32)).astype(bf16)
            g = jnp.dot(coef[...], jnp.concatenate([hi, hi, lo], axis=0), preferred_element_type=f32)
            for n in range(STEPS):
                for t in range(3):
                    total[t] = total[t] + e[n + 1, c, v, t] * g[8 * n : 8 * n + 8, LANES * t : LANES * t + LANES]
        for t in range(3):
            raw[v + 2, t] = total[t] * fst[PLANES, t, at, :]
        return 0

    lax.fori_loop(0, CHUNK, gather, 0)
    for t in range(3):
        for v in range(2):
            raw[v, t] = turn(raw[CHUNK + v, t], 1, 0)
            raw[CHUNK + 2 + v, t] = turn(raw[2 + v, t], -1, 0)

    table = filter_table()

    def smooth(v, _):
        part = []
        for t in range(3):
            r0 = raw[v + 2, t]
            r1 = raw[v + 1, t] + raw[v + 3, t]
            r2 = raw[v, t] + raw[v + 4, t]
            part.append([
                float(table[3, 3 + b]) * r0 + float(table[4, 3 + b]) * r1 + float(table[5, 3 + b]) * r2 for b in range(3)
            ])
        at = pl.ds(FIRST + v, 8, stride=CHUNK)
        for t in range(2):
            acc = part[t][0]
            for b in (1, 2):
                up = jnp.where(lane >= LANES - b, turn(part[(t + 1) % 3][b], -b, 1), turn(part[t][b], -b, 1))
                down = jnp.where(lane < b, turn(part[(t + 2) % 3][b], b, 1), turn(part[t][b], b, 1))
                acc = acc + (up + down)
            stage[6, t, at, :] = acc
        return 0

    lax.fori_loop(0, CHUNK, smooth, 0)
    stores += [
        pltpu.make_async_copy(stage.at[6, t, own], grad.at[:, pl.ds(LANES * t, LANES)], sems.at[2 + t]) for t in range(2)
    ]
    for copy in stores[2:]:
        copy.start()
    for copy in stores:
        copy.wait()


def advance(coef, fields, inv_eps, fwd, mask, *edges):
    any_space = pl.BlockSpec(memory_space=pl.ANY)
    return pl.pallas_call(
        main_kernel,
        out_shape=(jax.ShapeDtypeStruct((6, T, T), f32), jax.ShapeDtypeStruct((T, T), f32)),
        in_specs=[pl.BlockSpec(memory_space=pltpu.VMEM)] + [any_space] * 10,
        out_specs=(any_space,) * 2,
        scratch_shapes=[
            pltpu.VMEM((7, 3, ROWS, LANES), f32),
            pltpu.VMEM((PLANES + 1, 3, ROWS, LANES), f32),
            pltpu.VMEM((T, T), jnp.int32),
            pltpu.VMEM((7, 64, LANES), f32),
            pltpu.VMEM((7, 64, LANES), f32),
            pltpu.VMEM((7, 32, LANES), f32),
            pltpu.VMEM((7, 32, LANES), f32),
            pltpu.VMEM((STEPS + 1, 3, CHUNK, 3, 8, LANES), f32),
            pltpu.VMEM((3, CHUNK, 3, 8, LANES), f32),
            pltpu.VMEM((CHUNK, 3, 8, LANES), f32),
            pltpu.VMEM((CHUNK + 4, 3, 8, LANES), f32),
            pltpu.SemaphoreType.DMA((15,)),
        ],
        compiler_params=pltpu.CompilerParams(vmem_limit_bytes=58 * 2**20),
        name="advance",
    )(coef, fields, inv_eps, fwd, mask, *edges)


def swap(x, axis, offset):
    count = lax.axis_size(axis)
    route = []
    for i in range(offset, count + offset, 2):
        a, b = i % count, (i + 1) % count
        route += [(a, b), (b, a)]
    return lax.ppermute(x, axis, route)


def coefficients(phase_start, omega):
    theta = phase_start[None] + omega[None] * jnp.arange(STEPS, dtype=f32)[:, None]
    table = jnp.stack([jnp.cos(theta), -jnp.sin(theta)], axis=2).reshape(STEPS, 2 * NF) / STEPS
    high = lax.reduce_precision(table, 8, 7)
    low = lax.reduce_precision(table - high, 8, 7)
    cols = jnp.concatenate([high, low, high], axis=1)
    wide = cols[:, None, :, None] * jnp.eye(8, dtype=f32)[None, :, None, :]
    return wide.reshape(STEPS * 8, 3 * K).astype(bf16)


def local(fields, inv_eps, fwd_dft, phase_start, omega, mask):
    fwd = fwd_dft.reshape(PLANES, T, T)
    coef = coefficients(phase_start, omega)
    xs0, xs1, ys0, ys1 = pack(fields, inv_eps, fwd, mask)
    y0 = swap(ys0, "gy", 0)
    x0 = swap(xs0, "gx", 0)
    y1 = swap(ys1, "gy", 1)
    x1 = swap(xs1, "gx", 1)
    even_x = lax.rem(lax.axis_index("gx"), 2) == 0
    even_y = lax.rem(lax.axis_index("gy"), 2) == 0
    right = jnp.where(even_y, y0, y1)
    left = jnp.where(even_y, y1, y0)
    lane = lax.broadcasted_iota(jnp.int32, (7, 32, LANES), 2)
    up = jnp.where(lane >= 96, right[:, 32:], left[:, 32:])
    down = jnp.where(lane < 32, right[:, :32], left[:, :32])
    c0 = swap(jnp.where(even_x, up, down), "gx", 0)
    c1 = swap(jnp.where(even_x, down, up), "gx", 1)
    return advance(coef, fields, inv_eps, fwd, mask, x0, x1, y0, y1, c0, c1)


def solution(mesh):
    return jax.shard_map(
        local,
        mesh=mesh,
        in_specs=(
            P(None, "gx", "gy"),
            P("gx", "gy"),
            P(None, None, None, "gx", "gy"),
            P(),
            P(),
            P("gx", "gy"),
        ),
        out_specs=(P(None, "gx", "gy"), P("gx", "gy")),
        check_vma=False,
    )
```

```python
import functools

import jax
import jax.numpy as jnp
import numpy as np
from jax import lax
from jax.experimental import pallas as pl
from jax.experimental.pallas import tpu as pltpu
from jax.sharding import PartitionSpec as P

STEPS = 24
NF = 3
RADIUS = 3
COURANT = 0.68

T = 256
PAD = 32
ROWS = T + 2 * PAD
CHUNK = 39
FIRST = (ROWS - 8 * CHUNK) // 2
LANES = 128
DEEP = STEPS + 2
PLANES = 6 * NF
K = 8 * 2 * NF

f32 = jnp.float32
bf16 = jnp.bfloat16


def filter_table():
    offsets = np.arange(-RADIUS, RADIUS + 1)
    dist = np.sqrt(offsets[:, None] ** 2 + offsets[None, :] ** 2)
    table = np.maximum(0.0, RADIUS - dist)
    return table / table.sum()


def lane_iota():
    return lax.broadcasted_iota(jnp.int32, (8, LANES), 1)


def turn(x, shift, axis):
    size = x.shape[axis]
    shift = shift % size
    return x if shift == 0 else pltpu.roll(x, shift, axis)


def right_slot(group, k):
    return 32 * ((group + (2 if k >= 4 else 0)) % 4)


def left_slot(group, k):
    return 32 * ((group + (3 if k >= 4 else 1)) % 4)


def chunked(body, times):
    def several(i, _):
        for u in range(times):
            body(times * i + u)
        return 0

    lax.fori_loop(0, CHUNK // times, several, 0)


def riders(k):
    return [(jj, m) for jj, m in enumerate(range(3 * k, 3 * k + 3)) if m <= PLANES]


def pack_kernel(fields, inv_eps, fwd, mask, xs0, xs1, ys0, ys1, f7, fw, mk, sems):
    even_x = lax.rem(lax.axis_index("gx"), 2) == 0
    even_y = lax.rem(lax.axis_index("gy"), 2) == 0
    loads = [
        pltpu.make_async_copy(fields, f7.at[pl.ds(0, 6)], sems.at[0]),
        pltpu.make_async_copy(inv_eps, f7.at[6], sems.at[1]),
        pltpu.make_async_copy(mask, mk, sems.at[2]),
        pltpu.make_async_copy(fwd, fw.at[pl.ds(0, PLANES)], sems.at[3]),
    ]
    for copy in loads:
        copy.start()
    lane = lane_iota()
    sub = lax.broadcasted_iota(jnp.int32, (8, T), 0)

    def rows(ref, k, g, j, t):
        return ref[k, pl.ds(pl.multiple_of(64 * g + 8 * j, 8), 8), pl.ds(LANES * t, LANES)]

    def main(i, _):
        for j in (2 * i, 2 * i + 1):
            to = pl.ds(pl.multiple_of(8 * j, 8), 8)
            for k in range(7):
                first = last = None
                for g in range(4):
                    a = turn(rows(f7, k, g, j, 0), right_slot(g, k), 1)
                    b = turn(rows(f7, k, g, j, 1), left_slot(g, k) - 96, 1)
                    first = a if g == 0 else jnp.where(lane // 32 == right_slot(g, k) // 32, a, first)
                    last = b if g == 0 else jnp.where(lane // 32 == left_slot(g, k) // 32, b, last)
                ys0[k, to] = first
                ys1[k, to] = last
        return 0

    def ride(i, _):
        for j in (2 * i, 2 * i + 1):
            to = pl.ds(pl.multiple_of(8 * j, 8), 8)
            for k in range(7):
                first, last = ys0[k, to], ys1[k, to]
                for jj, m in riders(k):
                    for g in range(4):
                        a, b = right_slot(g, k) + 26 + 2 * jj, left_slot(g, k) + 2 * jj
                        first = jnp.where(lane // 2 == a // 2, turn(rows(fw, m, g, j, 0), a, 1), first)
                        last = jnp.where(lane // 2 == b // 2, turn(rows(fw, m, g, j, 1), b - 126, 1), last)
                ys0[k, to] = jnp.where(even_y, last, first)
                ys1[k, to] = jnp.where(even_y, first, last)
        return 0

    loads[0].wait()
    loads[1].wait()
    lax.fori_loop(0, 4, main, 0)
    loads[2].wait()
    fw[PLANES] = mk[...].astype(f32)
    loads[3].wait()
    lax.fori_loop(0, 4, ride, 0)
    for k in range(7):
        low, high = f7[k, pl.ds(T - 32, 8)], f7[k, pl.ds(24, 8)]
        for jj, m in riders(k):
            low = jnp.where(sub // 2 == jj, turn(fw[m, pl.ds(T - 8, 8)], 2 * jj + 2, 0), low)
            high = jnp.where(sub // 2 == jj + 1, turn(fw[m, pl.ds(0, 8)], 2 * jj + 2, 0), high)
        for j in range(4):
            a = low if j == 0 else f7[k, pl.ds(T - 32 + 8 * j, 8)]
            b = high if j == 3 else f7[k, pl.ds(8 * j, 8)]
            xs0[k, pl.ds(8 * j, 8)] = jnp.where(even_x, a, b)
            xs1[k, pl.ds(8 * j, 8)] = jnp.where(even_x, b, a)


def pack(fields, inv_eps, fwd, mask):
    x_slab = jax.ShapeDtypeStruct((7, 32, T), f32)
    y_slab = jax.ShapeDtypeStruct((7, 64, LANES), f32)
    return pl.pallas_call(
        pack_kernel,
        out_shape=(x_slab, x_slab, y_slab, y_slab),
        in_specs=[pl.BlockSpec(memory_space=pl.ANY)] * 4,
        out_specs=(pl.BlockSpec(memory_space=pltpu.VMEM),) * 4,
        scratch_shapes=[
            pltpu.VMEM((7, T, T), f32),
            pltpu.VMEM((PLANES + 1, T, T), f32),
            pltpu.VMEM((T, T), jnp.int32),
            pltpu.SemaphoreType.DMA((4,)),
        ],
        compiler_params=pltpu.CompilerParams(vmem_limit_bytes=56 * 2**20),
        name="pack",
    )(fields, inv_eps, fwd, mask)


def next_lane(tiles, lane):
    r = [turn(x, -1, 1) for x in tiles]
    return [jnp.where(lane == LANES - 1, r[(t + 1) % 3], r[t]) for t in range(3)]


def prev_lane(tiles, lane):
    r = [turn(x, 1, 1) for x in tiles]
    return [jnp.where(lane == 0, r[(t + 2) % 3], r[t]) for t in range(3)]


def main_kernel(table, fields, inv_eps, fwd, mask, y0, y1, x0, x1, c0, c1, out, grad,
                stage, fst, mk, yl, yr, cl, ch, coef, e, h, fac, raw, sems):
    px = lax.rem(lax.axis_index("gx"), 2)
    py = lax.rem(lax.axis_index("gy"), 2)
    own = pl.ds(PAD, T)
    copies, late = [], []
    for t in range(2):
        cols = pl.ds(LANES * t, LANES)
        copies.append(pltpu.make_async_copy(fields.at[:, :, cols], stage.at[pl.ds(0, 6), t, own], sems.at[t]))
        copies.append(pltpu.make_async_copy(inv_eps.at[:, cols], stage.at[6, t, own], sems.at[2 + t]))
        late.append(pltpu.make_async_copy(fwd.at[:, :, cols], fst.at[pl.ds(0, PLANES), t, own], sems.at[4 + t]))
    late.append(pltpu.make_async_copy(mask, mk, sems.at[6]))

    for copy in copies + late:
        copy.start()

    row = lax.broadcasted_iota(jnp.int32, (16, 3 * K), 0)
    col = lax.broadcasted_iota(jnp.int32, (16, 3 * K), 1)

    def spread(i, _):
        block = jnp.zeros((16, 3 * K), f32)
        for u in range(2):
            for j in range(6 * NF):
                block = jnp.where((row == col - 8 * j + 8 * u) & (col // 8 == j), table[2 * i + u, j], block)
        coef[pl.ds(pl.multiple_of(16 * i, 16), 16)] = block.astype(bf16)
        return 0

    lax.fori_loop(0, STEPS // 2, spread, 0)

    def deal(even, refs, to_low, to_high):
        @pl.when(even)
        def _():
            to_low(refs[1])
            to_high(refs[0])

        @pl.when(jnp.logical_not(even))
        def _():
            to_low(refs[0])
            to_high(refs[1])

    def into(ref):
        def copy(src):
            ref[...] = src[...]

        return copy

    def rim(row):
        def copy(src):
            for t in range(2):
                stage[:, t, pl.ds(row, PAD)] = src[:, :, pl.ds(LANES * t, LANES)]

        return copy

    deal(px == 0, (x0, x1), rim(0), rim(PAD + T))
    deal(py == 0, (y0, y1), into(yl), into(yr))
    deal(px == 0, (c0, c1), into(cl), into(ch))

    lane = lane_iota()
    sub = lax.broadcasted_iota(jnp.int32, (8, LANES), 0)
    right_half = lane < 64

    def fill(j, _):
        at = pl.ds(pl.multiple_of(8 * j, 8), 8)
        for k in range(7):
            r, l = yr[k, at], yl[k, at]
            for g in range(4):
                to = pl.ds(pl.multiple_of(PAD + 64 * g + 8 * j, 8), 8)
                stage[k, 2, to] = jnp.where(
                    right_half, turn(r, -right_slot(g, k), 1), turn(l, 96 - left_slot(g, k), 1)
                )
                for jj, m in enumerate(range(3 * k, min(3 * k + 3, PLANES + 1))):
                    fst[m, 2, to] = jnp.where(
                        right_half,
                        turn(r, -right_slot(g, k) - 26 - 2 * jj, 1),
                        turn(l, 126 - left_slot(g, k) - 2 * jj, 1),
                    )
        return 0

    lax.fori_loop(0, 8, fill, 0)
    zero = jnp.zeros((8, LANES), f32)
    for k in range(7):
        c = k % 4
        rl, ll, rh, lh = right_slot(3, k), left_slot(3, k), right_slot(0, k), left_slot(0, k)
        for j in range(4):
            a, b = cl[c, pl.ds(8 * j, 8)], ch[c, pl.ds(8 * j, 8)]
            stage[k, 2, pl.ds(8 * j, 8)] = jnp.where(right_half, turn(a, -rl, 1), turn(a, 96 - ll, 1))
            stage[k, 2, pl.ds(PAD + T + 8 * j, 8)] = jnp.where(right_half, turn(b, -rh, 1), turn(b, 96 - lh, 1))
        a, b = cl[c, pl.ds(24, 8)], ch[c, pl.ds(0, 8)]
        for jj, m in riders(k):
            fst[m, 2, pl.ds(24, 8)] = jnp.where(
                right_half, turn(a, -rl - 26 - 2 * jj, 1), turn(a, 126 - ll - 2 * jj, 1)
            )
            fst[m, 2, pl.ds(PAD + T, 8)] = jnp.where(
                right_half, turn(b, -rh - 26 - 2 * jj, 1), turn(b, 126 - lh - 2 * jj, 1)
            )
            for t in range(2):
                lo, hi = stage[k, t, pl.ds(0, 8)], stage[k, t, pl.ds(ROWS - 8, 8)]
                fst[m, t, pl.ds(24, 8)] = jnp.where(sub >= 6, turn(lo, 6 - 2 * jj, 0), 0.0)
                fst[m, t, pl.ds(PAD + T, 8)] = jnp.where(sub < 2, turn(hi, -2 - 2 * jj, 0), 0.0)
            for t in range(3):
                for j in range(3):
                    fst[m, t, pl.ds(8 * j, 8)] = zero
                    fst[m, t, pl.ds(PAD + T + 8 + 8 * j, 8)] = zero

    def lift(v):
        at = pl.ds(FIRST + v, 8, stride=CHUNK)
        for t in range(3):
            for c in range(3):
                e[0, c, v, t] = stage[c, t, at, :]
                h[c, v, t] = stage[3 + c, t, at, :] * (1.0 / COURANT)
            fac[v, t] = stage[6, t, at, :] * (COURANT * COURANT)

    for copy in copies:
        copy.wait()
    chunked(lift, 3)

    def put(ref, tiles, v):
        for t in range(3):
            ref[v, t] = tiles[t]

    def get(ref, v):
        return [ref[v, t] for t in range(3)]

    def step(n, _):
        old, new = e.at[n], e.at[n + 1]
        ey, ez = get(old.at[1], 0), get(old.at[2], 0)
        end = ([turn(x, -1, 0) for x in ey], [turn(x, -1, 0) for x in ez])
        for v in range(CHUNK):
            ey_n, ez_n = (get(old.at[1], v + 1), get(old.at[2], v + 1)) if v < CHUNK - 1 else end
            ex = get(old.at[0], v)
            xn, zn = next_lane(ex, lane), next_lane(ez, lane)
            hx, hy, hz = get(h.at[0], v), get(h.at[1], v), get(h.at[2], v)
            for t in range(3):
                hx[t] = hx[t] - (zn[t] - ez[t])
                hy[t] = hy[t] + (ez_n[t] - ez[t])
                hz[t] = hz[t] - ((ey_n[t] - ey[t]) - (xn[t] - ex[t]))
            put(h.at[0], hx, v)
            put(h.at[1], hy, v)
            put(h.at[2], hz, v)
            ey, ez = ey_n, ez_n
        hy_p, hz_p = [turn(x, 1, 0) for x in hy], [turn(x, 1, 0) for x in hz]
        for v in range(CHUNK):
            hx, hy, hz = get(h.at[0], v), get(h.at[1], v), get(h.at[2], v)
            xp, zp, f = prev_lane(hx, lane), prev_lane(hz, lane), get(fac, v)
            ex, ey, ez = get(old.at[0], v), get(old.at[1], v), get(old.at[2], v)
            for t in range(3):
                ex[t] = ex[t] + f[t] * (hz[t] - zp[t])
                ey[t] = ey[t] - f[t] * (hz[t] - hz_p[t])
                ez[t] = ez[t] + f[t] * ((hy[t] - hy_p[t]) - (hx[t] - xp[t]))
            put(new.at[0], ex, v)
            put(new.at[1], ey, v)
            put(new.at[2], ez, v)
            hy_p, hz_p = hy, hz
        return 0

    lax.fori_loop(0, STEPS // 2, lambda i, _: step(2 * i + 1, step(2 * i, 0)), 0)

    for copy in late:
        copy.wait()
    for t in range(2):
        fst[PLANES, t, own] = mk[:, pl.ds(LANES * t, LANES)].astype(f32)

    def lower(v):
        at = pl.ds(FIRST + v, 8, stride=CHUNK)
        for t in range(2):
            for c in range(3):
                stage[c, t, at, :] = e[STEPS, c, v, t]
                stage[3 + c, t, at, :] = h[c, v, t] * COURANT

    chunked(lower, 3)
    stores = [
        pltpu.make_async_copy(stage.at[pl.ds(0, 6), t, own], out.at[:, :, pl.ds(LANES * t, LANES)], sems.at[t])
        for t in range(2)
    ]
    for copy in stores:
        copy.start()

    def gather(v):
        at = pl.ds(FIRST + v, 8, stride=CHUNK)
        total = [zero] * 3
        for c in range(3):
            w = jnp.concatenate(
                [jnp.concatenate([fst[3 * i + c, t, at, :] for t in range(3)], axis=1) for i in range(2 * NF)], axis=0
            )
            hi = w.astype(bf16)
            lo = (w - hi.astype(f32)).astype(bf16)
            g = jnp.dot(coef[...], jnp.concatenate([hi, hi, lo], axis=0), preferred_element_type=f32)
            for n in range(STEPS):
                for t in range(3):
                    total[t] = total[t] + e[n + 1, c, v, t] * g[8 * n : 8 * n + 8, LANES * t : LANES * t + LANES]
        for t in range(3):
            raw[v + 2, t] = total[t] * fst[PLANES, t, at, :]

    chunked(gather, 13)
    for t in range(3):
        for v in range(2):
            raw[v, t] = turn(raw[CHUNK + v, t], 1, 0)
            raw[CHUNK + 2 + v, t] = turn(raw[2 + v, t], -1, 0)

    taps = filter_table()

    def smooth(v):
        part = []
        for t in range(3):
            r0 = raw[v + 2, t]
            r1 = raw[v + 1, t] + raw[v + 3, t]
            r2 = raw[v, t] + raw[v + 4, t]
            part.append([
                float(taps[3, 3 + b]) * r0 + float(taps[4, 3 + b]) * r1 + float(taps[5, 3 + b]) * r2 for b in range(3)
            ])
        at = pl.ds(FIRST + v, 8, stride=CHUNK)
        for t in range(2):
            acc = part[t][0]
            for b in (1, 2):
                up = jnp.where(lane >= LANES - b, turn(part[(t + 1) % 3][b], -b, 1), turn(part[t][b], -b, 1))
                down = jnp.where(lane < b, turn(part[(t + 2) % 3][b], b, 1), turn(part[t][b], b, 1))
                acc = acc + (up + down)
            stage[6, t, at, :] = acc

    chunked(smooth, 13)
    stores += [
        pltpu.make_async_copy(stage.at[6, t, own], grad.at[:, pl.ds(LANES * t, LANES)], sems.at[2 + t]) for t in range(2)
    ]
    for copy in stores[2:]:
        copy.start()
    for copy in stores:
        copy.wait()


def advance(table, fields, inv_eps, fwd, mask, *edges):
    vmem = pl.BlockSpec(memory_space=pltpu.VMEM)
    any_space = pl.BlockSpec(memory_space=pl.ANY)
    return pl.pallas_call(
        main_kernel,
        out_shape=(jax.ShapeDtypeStruct((6, T, T), f32), jax.ShapeDtypeStruct((T, T), f32)),
        in_specs=[pl.BlockSpec(memory_space=pltpu.SMEM)] + [any_space] * 4 + [vmem] * 6,
        out_specs=(any_space,) * 2,
        scratch_shapes=[
            pltpu.VMEM((7, 3, ROWS, LANES), f32),
            pltpu.VMEM((PLANES + 1, 3, ROWS, LANES), f32),
            pltpu.VMEM((T, T), jnp.int32),
            pltpu.VMEM((7, 64, LANES), f32),
            pltpu.VMEM((7, 64, LANES), f32),
            pltpu.VMEM((4, 32, LANES), f32),
            pltpu.VMEM((4, 32, LANES), f32),
            pltpu.VMEM((2 * STEPS * 4, 3 * K), bf16),
            pltpu.VMEM((STEPS + 1, 3, CHUNK, 3, 8, LANES), f32),
            pltpu.VMEM((3, CHUNK, 3, 8, LANES), f32),
            pltpu.VMEM((CHUNK, 3, 8, LANES), f32),
            pltpu.VMEM((CHUNK + 4, 3, 8, LANES), f32),
            pltpu.SemaphoreType.DMA((7,)),
        ],
        compiler_params=pltpu.CompilerParams(vmem_limit_bytes=58 * 2**20),
        name="advance",
    )(table, fields, inv_eps, fwd, mask, *edges)


def swap(x, axis, offset):
    count = lax.axis_size(axis)
    route = []
    for i in range(offset, count + offset, 2):
        a, b = i % count, (i + 1) % count
        route += [(a, b), (b, a)]
    return lax.ppermute(x, axis, route)


def coefficients(phase_start, omega):
    theta = phase_start[None] + omega[None] * jnp.arange(STEPS, dtype=f32)[:, None]
    table = jnp.stack([jnp.cos(theta), -jnp.sin(theta)], axis=2).reshape(STEPS, 2 * NF) / STEPS
    high = lax.reduce_precision(table, 8, 7)
    low = lax.reduce_precision(table - high, 8, 7)
    return jnp.concatenate([high, low, high], axis=1)


def local(fields, inv_eps, fwd_dft, phase_start, omega, mask):
    fwd = fwd_dft.reshape(PLANES, T, T)
    table = coefficients(phase_start, omega)
    xs0, xs1, ys0, ys1 = pack(fields, inv_eps, fwd, mask)
    y0 = swap(ys0, "gy", 0)
    y1 = swap(ys1, "gy", 1)
    x0 = swap(xs0, "gx", 0)
    x1 = swap(xs1, "gx", 1)
    even_x = lax.rem(lax.axis_index("gx"), 2) == 0
    even_y = lax.rem(lax.axis_index("gy"), 2) == 0
    right = jnp.where(even_y, y0, y1)
    left = jnp.where(even_y, y1, y0)
    lane = lax.broadcasted_iota(jnp.int32, (4, 32, LANES), 2)

    def corner(rows, group):
        r, l = right[:, rows], left[:, rows]
        r4, l4 = jnp.concatenate([r[4:], r[:1]]), jnp.concatenate([l[4:], l[:1]])
        block = lane // 32 * 32
        res = jnp.where(block == right_slot(group, 0), r[:4], l[:4])
        res = jnp.where(block == right_slot(group, 4), r4, res)
        return jnp.where(block == left_slot(group, 4), l4, res)

    up, down = corner(slice(32, 64), 3), corner(slice(0, 32), 0)
    c0 = swap(jnp.where(even_x, up, down), "gx", 0)
    c1 = swap(jnp.where(even_x, down, up), "gx", 1)
    return advance(table, fields, inv_eps, fwd, mask, y0, y1, x0, x1, c0, c1)


def solution(mesh):
    return jax.shard_map(
        local,
        mesh=mesh,
        in_specs=(
            P(None, "gx", "gy"),
            P("gx", "gy"),
            P(None, None, None, "gx", "gy"),
            P(),
            P(),
            P("gx", "gy"),
        ),
        out_specs=(P(None, "gx", "gy"), P("gx", "gy")),
        check_vma=False,
    )
```

```python
import functools

import jax
import jax.numpy as jnp
import numpy as np
from jax import lax
from jax.experimental import pallas as pl
from jax.experimental.pallas import tpu as pltpu
from jax.sharding import PartitionSpec as P

STEPS = 24
NF = 3
RADIUS = 3
COURANT = 0.68

T = 256
PAD = 32
ROWS = T + 2 * PAD
CHUNK = ROWS // 8
HALF = CHUNK // 2
LANES = 128
UNROLL = 6
PLANES = 6 * NF
K = 8 * 2 * NF

f32 = jnp.float32
bf16 = jnp.bfloat16


def filter_table():
    offsets = np.arange(-RADIUS, RADIUS + 1)
    dist = np.sqrt(offsets[:, None] ** 2 + offsets[None, :] ** 2)
    table = np.maximum(0.0, RADIUS - dist)
    return table / table.sum()


def lane_iota():
    return lax.broadcasted_iota(jnp.int32, (8, LANES), 1)


def turn(x, shift, axis):
    size = x.shape[axis]
    shift = shift % size
    return x if shift == 0 else pltpu.roll(x, shift, axis)


def right_slot(group, k):
    return 32 * ((group + (2 if k >= 4 else 0)) % 4)


def left_slot(group, k):
    return 32 * ((group + (3 if k >= 4 else 1)) % 4)


def chunked(body, times):
    def several(i, _):
        for u in range(times):
            body(times * i + u)
        return 0

    lax.fori_loop(0, HALF // times, several, 0)


def riders(k):
    return [(jj, m) for jj, m in enumerate(range(3 * k, 3 * k + 3)) if m <= PLANES]


def x_slab(side, plane, rider, write):
    sub = lax.broadcasted_iota(jnp.int32, (8, T), 0)
    for k in range(7):
        edge = plane(k, 0 if side == 0 else 24)
        for jj, m in riders(k):
            edge = jnp.where(sub // 2 == jj + side, turn(rider(m), 2 * jj + 2, 0), edge)
        for j in range(4):
            write(k, 8 * j, edge if j == 3 * side else plane(k, 8 * j))


def pack_kernel(fields, inv_eps, fwd, mask, xs0, xs1, ys0, ys1, f7, fw, mk, sems):
    even_x = lax.rem(lax.axis_index("gx"), 2) == 0
    even_y = lax.rem(lax.axis_index("gy"), 2) == 0
    loads = [
        pltpu.make_async_copy(fields, f7.at[pl.ds(0, 6)], sems.at[0]),
        pltpu.make_async_copy(inv_eps, f7.at[6], sems.at[1]),
        pltpu.make_async_copy(mask, mk, sems.at[2]),
    ]
    loads += [
        pltpu.make_async_copy(fwd.at[pl.ds(3 * k, 3)], fw.at[pl.ds(3 * k, 3)], sems.at[3 + k]) for k in range(6)
    ]
    for copy in loads:
        copy.start()
    lane = lane_iota()

    def rows(ref, k, g, j, t):
        return ref[k, pl.ds(64 * g + 8 * j, 8), pl.ds(LANES * t, LANES)]

    loads[0].wait()
    loads[1].wait()
    for k in (6, 0, 1, 2, 3, 4, 5):
        if k == 6:
            loads[2].wait()
            fw[PLANES] = mk[...].astype(f32)
        else:
            loads[3 + k].wait()
        for j in range(8):
            first = last = None
            for g in range(4):
                a = turn(rows(f7, k, g, j, 0), right_slot(g, k), 1)
                b = turn(rows(f7, k, g, j, 1), left_slot(g, k) - 96, 1)
                first = a if g == 0 else jnp.where(lane // 32 == right_slot(g, k) // 32, a, first)
                last = b if g == 0 else jnp.where(lane // 32 == left_slot(g, k) // 32, b, last)
            for jj, m in riders(k):
                for g in range(4):
                    a, b = right_slot(g, k) + 26 + 2 * jj, left_slot(g, k) + 2 * jj
                    first = jnp.where(lane // 2 == a // 2, turn(rows(fw, m, g, j, 0), a, 1), first)
                    last = jnp.where(lane // 2 == b // 2, turn(rows(fw, m, g, j, 1), b - 126, 1), last)
            to = pl.ds(8 * j, 8)
            ys0[k, to] = jnp.where(even_y, last, first)
            ys1[k, to] = jnp.where(even_y, first, last)

    def write(side):
        def put_row(k, row, value):
            if side == 0:
                xs0[k, pl.ds(row, 8)] = value
            else:
                xs1[k, pl.ds(row, 8)] = value

        return put_row

    for flip, here in ((0, even_x), (1, jnp.logical_not(even_x))):
        @pl.when(here)
        def _():
            for side, (base, near) in enumerate(((T - 32, T - 8), (0, 0))):
                x_slab(
                    side,
                    lambda k, row: f7[k, pl.ds(base + row, 8)],
                    lambda m: fw[m, pl.ds(near, 8)],
                    write(side ^ flip),
                )


def pack(fields, inv_eps, fwd, mask):
    x_shape = jax.ShapeDtypeStruct((7, 32, T), f32)
    y_shape = jax.ShapeDtypeStruct((7, 64, LANES), f32)
    return pl.pallas_call(
        pack_kernel,
        out_shape=(x_shape, x_shape, y_shape, y_shape),
        in_specs=[pl.BlockSpec(memory_space=pl.ANY)] * 4,
        out_specs=(pl.BlockSpec(memory_space=pltpu.VMEM),) * 4,
        scratch_shapes=[
            pltpu.VMEM((7, T, T), f32),
            pltpu.VMEM((PLANES + 1, T, T), f32),
            pltpu.VMEM((T, T), jnp.int32),
            pltpu.SemaphoreType.DMA((9,)),
        ],
        compiler_params=pltpu.CompilerParams(vmem_limit_bytes=56 * 2**20),
        cost_estimate=pl.CostEstimate(flops=10**7, bytes_accessed=7 * 10**6, transcendentals=0),
        name="pack",
    )(fields, inv_eps, fwd, mask)


def half_turn(x):
    return turn(x, LANES // 2, 1)


def next_lane(q, lane, by=1):
    a0, a1, b0, b1, x = [turn(z, -by, 1) for z in q]
    end, mid = lane >= LANES - by, (lane >= 64 - by) & (lane < 64)
    return [
        jnp.where(end, a1, a0),
        jnp.where(end, x, a1),
        jnp.where(mid, b1, b0),
        jnp.where(mid, x, b1),
        jnp.where(end, a0, jnp.where(mid, b0, x)),
    ]


def prev_lane(q, lane, by=1):
    a0, a1, b0, b1, x = [turn(z, by, 1) for z in q]
    end, mid = lane < by, (lane >= 64) & (lane < 64 + by)
    return [
        jnp.where(end, x, a0),
        jnp.where(end, a0, a1),
        jnp.where(mid, x, b0),
        jnp.where(mid, b0, b1),
        jnp.where(end, a1, jnp.where(mid, b1, x)),
    ]


def of_first(lane):
    return (lane < 32) | (lane >= 96)


def wrap_next(q, lane):
    a0, a1, b0, b1, x = [half_turn(z) for z in q]
    return [b0, b1, turn(a0, -1, 0), turn(a1, -1, 0), jnp.where(of_first(lane), x, turn(x, -1, 0))]


def wrap_prev(q, lane):
    a0, a1, b0, b1, x = [half_turn(z) for z in q]
    return [turn(b0, 1, 0), turn(b1, 1, 0), a0, a1, jnp.where(of_first(lane), turn(x, 1, 0), x)]


def load_pair(plane, u, lane):
    v, w = pl.ds(u, 8, stride=CHUNK), pl.ds(u + HALF, 8, stride=CHUNK)
    res = [plane(t)[v, :] for t in range(2)] + [half_turn(plane(t)[w, :]) for t in range(2)]
    return res + [jnp.where(of_first(lane), plane(2)[v, :], half_turn(plane(2)[w, :]))]


def store_pair(plane, u, q):
    v, w = pl.ds(u, 8, stride=CHUNK), pl.ds(u + HALF, 8, stride=CHUNK)
    for t in range(2):
        plane(t)[v, :] = q[t]
        plane(t)[w, :] = half_turn(q[2 + t])


def main_kernel(table, fields, inv_eps, fwd, mask, y0, y1, x0, x1, c0, c1, out, grad,
                stage, fst, mk, yl, yr, cl, ch, coef, e, h, fac, raw, sems):
    px = lax.rem(lax.axis_index("gx"), 2)
    py = lax.rem(lax.axis_index("gy"), 2)
    own = pl.ds(PAD, T)
    copies, late = [], []
    for t in range(2):
        cols = pl.ds(LANES * t, LANES)
        copies.append(pltpu.make_async_copy(fields.at[:, :, cols], stage.at[pl.ds(0, 6), t, own], sems.at[t]))
        copies.append(pltpu.make_async_copy(inv_eps.at[:, cols], stage.at[6, t, own], sems.at[2 + t]))
        late.append(pltpu.make_async_copy(fwd.at[:, :, cols], fst.at[pl.ds(0, PLANES), t, own], sems.at[4 + t]))
    late.append(pltpu.make_async_copy(mask, mk, sems.at[6]))

    def edges(low, high, left, right, clow, chigh):
        res = []
        for t in range(2):
            cols = pl.ds(LANES * t, LANES)
            res.append(pltpu.make_async_copy(low.at[:, :, cols], stage.at[:, t, pl.ds(0, PAD)], sems.at[7 + t]))
            res.append(pltpu.make_async_copy(high.at[:, :, cols], stage.at[:, t, pl.ds(PAD + T, PAD)], sems.at[9 + t]))
        res.append(pltpu.make_async_copy(left, yl, sems.at[11]))
        res.append(pltpu.make_async_copy(right, yr, sems.at[12]))
        res.append(pltpu.make_async_copy(clow, cl, sems.at[13]))
        res.append(pltpu.make_async_copy(chigh, ch, sems.at[14]))
        return res

    for ix in range(2):
        for iy in range(2):
            @pl.when((px == ix) & (py == iy))
            def _():
                xs = (x1, x0) if ix == 0 else (x0, x1)
                ys = (y1, y0) if iy == 0 else (y0, y1)
                cs = (c1, c0) if ix == 0 else (c0, c1)
                for copy in edges(*xs, *ys, *cs):
                    copy.start()
    for copy in copies + late:
        copy.start()

    row = lax.broadcasted_iota(jnp.int32, (16, 3 * K), 0)
    col = lax.broadcasted_iota(jnp.int32, (16, 3 * K), 1)

    def spread(i, _):
        block = jnp.zeros((16, 3 * K), f32)
        for u in range(2):
            for j in range(6 * NF):
                block = jnp.where((row == col - 8 * j + 8 * u) & (col // 8 == j), table[2 * i + u, j], block)
        coef[pl.ds(pl.multiple_of(16 * i, 16), 16)] = block.astype(bf16)
        return 0

    lax.fori_loop(0, STEPS // 2, spread, 0)

    for copy in edges(x0, x1, y0, y1, c0, c1):
        copy.wait()

    lane = lane_iota()
    sub = lax.broadcasted_iota(jnp.int32, (8, LANES), 0)
    right_half = lane < 64

    def fill(j, _):
        at = pl.ds(pl.multiple_of(8 * j, 8), 8)
        for k in range(7):
            r, l = yr[k, at], yl[k, at]
            for g in range(4):
                to = pl.ds(pl.multiple_of(PAD + 64 * g + 8 * j, 8), 8)
                stage[k, 2, to] = jnp.where(
                    right_half, turn(r, -right_slot(g, k), 1), turn(l, 96 - left_slot(g, k), 1)
                )
                for jj, m in enumerate(range(3 * k, min(3 * k + 3, PLANES + 1))):
                    fst[m, 2, to] = jnp.where(
                        right_half,
                        turn(r, -right_slot(g, k) - 26 - 2 * jj, 1),
                        turn(l, 126 - left_slot(g, k) - 2 * jj, 1),
                    )
        return 0

    lax.fori_loop(0, 8, fill, 0)
    zero = jnp.zeros((8, LANES), f32)
    for k in range(7):
        c = k % 4
        rl, ll, rh, lh = right_slot(3, k), left_slot(3, k), right_slot(0, k), left_slot(0, k)
        for j in range(4):
            a, b = cl[c, pl.ds(8 * j, 8)], ch[c, pl.ds(8 * j, 8)]
            stage[k, 2, pl.ds(8 * j, 8)] = jnp.where(right_half, turn(a, -rl, 1), turn(a, 96 - ll, 1))
            stage[k, 2, pl.ds(PAD + T + 8 * j, 8)] = jnp.where(right_half, turn(b, -rh, 1), turn(b, 96 - lh, 1))
        a, b = cl[c, pl.ds(24, 8)], ch[c, pl.ds(0, 8)]
        for jj, m in riders(k):
            fst[m, 2, pl.ds(24, 8)] = jnp.where(
                right_half, turn(a, -rl - 26 - 2 * jj, 1), turn(a, 126 - ll - 2 * jj, 1)
            )
            fst[m, 2, pl.ds(PAD + T, 8)] = jnp.where(
                right_half, turn(b, -rh - 26 - 2 * jj, 1), turn(b, 126 - lh - 2 * jj, 1)
            )
            for t in range(2):
                lo, hi = stage[k, t, pl.ds(0, 8)], stage[k, t, pl.ds(ROWS - 8, 8)]
                fst[m, t, pl.ds(24, 8)] = jnp.where(sub >= 6, turn(lo, 6 - 2 * jj, 0), 0.0)
                fst[m, t, pl.ds(PAD + T, 8)] = jnp.where(sub < 2, turn(hi, -2 - 2 * jj, 0), 0.0)
            for t in range(3):
                for j in range(3):
                    fst[m, t, pl.ds(8 * j, 8)] = zero
                    fst[m, t, pl.ds(PAD + T + 8 + 8 * j, 8)] = zero

    def staged(ref, k):
        return lambda t: ref.at[k, t]

    def put(ref, q, u):
        for i in range(5):
            ref[u, i] = q[i]

    def get(ref, u):
        return [ref[u, i] for i in range(5)]

    def lift(u):
        for c in range(3):
            put(e.at[0, c], load_pair(staged(stage, c), u, lane), u)
            put(h.at[c], [z * (1.0 / COURANT) for z in load_pair(staged(stage, 3 + c), u, lane)], u)
        put(fac, [z * (COURANT * COURANT) for z in load_pair(staged(stage, 6), u, lane)], u)

    for copy in copies:
        copy.wait()
    chunked(lift, 10)

    def step(n, first):
        old, new = e.at[n], e.at[n + 1]

        def after(c, u):
            return get(old.at[c], u + 1) if u < HALF - 1 else wrap_next(get(old.at[c], 0), lane)

        ey, ez = get(old.at[1], first), get(old.at[2], first)
        for k in range(HALF):
            u = (first + k) % HALF
            if u == 0 and k > 0:
                ey, ez = get(old.at[1], 0), get(old.at[2], 0)
            ex, ey_n, ez_n = get(old.at[0], u), after(1, u), after(2, u)
            xn, zn = next_lane(ex, lane), next_lane(ez, lane)
            hx, hy, hz = get(h.at[0], u), get(h.at[1], u), get(h.at[2], u)
            for i in range(5):
                hx[i] = hx[i] - (zn[i] - ez[i])
                hy[i] = hy[i] + (ez_n[i] - ez[i])
                hz[i] = hz[i] - ((ey_n[i] - ey[i]) - (xn[i] - ex[i]))
            put(h.at[0], hx, u)
            put(h.at[1], hy, u)
            put(h.at[2], hz, u)
            ey, ez = ey_n, ez_n
        hy_p, hz_p = get(h.at[1], first), get(h.at[2], first)
        for k in range(HALF):
            u = (first + 1 + k) % HALF
            if u == 0:
                hy_p, hz_p = wrap_prev(hy_p, lane), wrap_prev(hz_p, lane)
            hx, hy, hz = get(h.at[0], u), get(h.at[1], u), get(h.at[2], u)
            xp, zp, f = prev_lane(hx, lane), prev_lane(hz, lane), get(fac, u)
            ex, ey, ez = get(old.at[0], u), get(old.at[1], u), get(old.at[2], u)
            for i in range(5):
                ex[i] = ex[i] + f[i] * (hz[i] - zp[i])
                ey[i] = ey[i] - f[i] * (hz[i] - hz_p[i])
                ez[i] = ez[i] + f[i] * ((hy[i] - hy_p[i]) - (hx[i] - xp[i]))
            put(new.at[0], ex, u)
            put(new.at[1], ey, u)
            put(new.at[2], ez, u)
            hy_p, hz_p = hy, hz

    def steps(i, _):
        for k in range(UNROLL):
            step(UNROLL * i + k, k)
        return 0

    lax.fori_loop(0, STEPS // UNROLL, steps, 0)

    for copy in late:
        copy.wait()
    for t in range(2):
        fst[PLANES, t, own] = mk[:, pl.ds(LANES * t, LANES)].astype(f32)

    def lower(u):
        for c in range(3):
            store_pair(staged(stage, c), u, get(e.at[STEPS, c], u))
            store_pair(staged(stage, 3 + c), u, [z * COURANT for z in get(h.at[c], u)])

    chunked(lower, 10)
    stores = [
        pltpu.make_async_copy(stage.at[pl.ds(0, 6), t, own], out.at[:, :, pl.ds(LANES * t, LANES)], sems.at[t])
        for t in range(2)
    ]
    for copy in stores:
        copy.start()

    def gather(u):
        total = [zero] * 5
        for c in range(3):
            w = jnp.concatenate(
                [jnp.concatenate(load_pair(staged(fst, 3 * i + c), u, lane), axis=1) for i in range(2 * NF)], axis=0
            )
            hi = w.astype(bf16)
            lo = (w - hi.astype(f32)).astype(bf16)
            g = jnp.dot(coef[...], jnp.concatenate([hi, hi, lo], axis=0), preferred_element_type=f32)
            for n in range(STEPS):
                for i in range(5):
                    total[i] = total[i] + e[n + 1, c, u, i] * g[8 * n : 8 * n + 8, LANES * i : LANES * i + LANES]
        part = load_pair(staged(fst, PLANES), u, lane)
        put(raw, [total[i] * part[i] for i in range(5)], u + 2)

    chunked(gather, 10)
    for i in range(2):
        put(raw, wrap_prev(get(raw, HALF + i), lane), i)
        put(raw, wrap_next(get(raw, 2 + i), lane), HALF + 2 + i)

    taps = filter_table()

    def smooth(u):
        part = [[], [], []]
        for i in range(5):
            r0 = raw[u + 2, i]
            r1 = raw[u + 1, i] + raw[u + 3, i]
            r2 = raw[u, i] + raw[u + 4, i]
            for b in range(3):
                part[b].append(float(taps[3, 3 + b]) * r0 + float(taps[4, 3 + b]) * r1 + float(taps[5, 3 + b]) * r2)
        acc = part[0]
        for b in (1, 2):
            up, down = next_lane(part[b], lane, b), prev_lane(part[b], lane, b)
            acc = [acc[i] + (up[i] + down[i]) for i in range(4)]
        store_pair(staged(stage, 6), u, acc)

    chunked(smooth, 10)
    stores += [
        pltpu.make_async_copy(stage.at[6, t, own], grad.at[:, pl.ds(LANES * t, LANES)], sems.at[2 + t]) for t in range(2)
    ]
    for copy in stores[2:]:
        copy.start()
    for copy in stores:
        copy.wait()


def advance(table, fields, inv_eps, fwd, mask, *edges):
    any_space = pl.BlockSpec(memory_space=pl.ANY)
    return pl.pallas_call(
        main_kernel,
        out_shape=(jax.ShapeDtypeStruct((6, T, T), f32), jax.ShapeDtypeStruct((T, T), f32)),
        in_specs=[pl.BlockSpec(memory_space=pltpu.SMEM)] + [any_space] * 10,
        out_specs=(any_space,) * 2,
        scratch_shapes=[
            pltpu.VMEM((7, 3, ROWS, LANES), f32),
            pltpu.VMEM((PLANES + 1, 3, ROWS, LANES), f32),
            pltpu.VMEM((T, T), jnp.int32),
            pltpu.VMEM((7, 64, LANES), f32),
            pltpu.VMEM((7, 64, LANES), f32),
            pltpu.VMEM((4, 32, LANES), f32),
            pltpu.VMEM((4, 32, LANES), f32),
            pltpu.VMEM((2 * STEPS * 4, 3 * K), bf16),
            pltpu.VMEM((STEPS + 1, 3, HALF, 5, 8, LANES), f32),
            pltpu.VMEM((3, HALF, 5, 8, LANES), f32),
            pltpu.VMEM((HALF, 5, 8, LANES), f32),
            pltpu.VMEM((HALF + 4, 5, 8, LANES), f32),
            pltpu.SemaphoreType.DMA((15,)),
        ],
        compiler_params=pltpu.CompilerParams(vmem_limit_bytes=48 * 2**20),
        name="advance",
    )(table, fields, inv_eps, fwd, mask, *edges)


def swap(x, axis, offset):
    count = lax.axis_size(axis)
    route = []
    for i in range(offset, count + offset, 2):
        a, b = i % count, (i + 1) % count
        route += [(a, b), (b, a)]
    return lax.ppermute(x, axis, route)


def coefficients(phase_start, omega):
    theta = phase_start[None] + omega[None] * jnp.arange(STEPS, dtype=f32)[:, None]
    table = jnp.stack([jnp.cos(theta), -jnp.sin(theta)], axis=2).reshape(STEPS, 2 * NF) / STEPS
    high = lax.reduce_precision(table, 8, 7)
    low = lax.reduce_precision(table - high, 8, 7)
    return jnp.concatenate([high, low, high], axis=1)


def local(fields, inv_eps, fwd_dft, phase_start, omega, mask):
    fwd = fwd_dft.reshape(PLANES, T, T)
    table = coefficients(phase_start, omega)
    xs0, xs1, ys0, ys1 = pack(fields, inv_eps, fwd, mask)
    y0 = swap(ys0, "gy", 0)
    y1 = swap(ys1, "gy", 1)
    x0 = swap(xs0, "gx", 0)
    x1 = swap(xs1, "gx", 1)
    even_x = lax.rem(lax.axis_index("gx"), 2) == 0
    even_y = lax.rem(lax.axis_index("gy"), 2) == 0
    right = jnp.where(even_y, y0, y1)
    left = jnp.where(even_y, y1, y0)
    lane = lax.broadcasted_iota(jnp.int32, (4, 32, LANES), 2)

    def corner(rows, group):
        r, l = right[:, rows], left[:, rows]
        r4, l4 = jnp.concatenate([r[4:], r[:1]]), jnp.concatenate([l[4:], l[:1]])
        block = lane // 32 * 32
        res = jnp.where(block == right_slot(group, 0), r[:4], l[:4])
        res = jnp.where(block == right_slot(group, 4), r4, res)
        return jnp.where(block == left_slot(group, 4), l4, res)

    up, down = corner(slice(32, 64), 3), corner(slice(0, 32), 0)
    c0 = swap(jnp.where(even_x, up, down), "gx", 0)
    c1 = swap(jnp.where(even_x, down, up), "gx", 1)
    return advance(table, fields, inv_eps, fwd, mask, y0, y1, x0, x1, c0, c1)


def solution(mesh):
    return jax.shard_map(
        local,
        mesh=mesh,
        in_specs=(
            P(None, "gx", "gy"),
            P("gx", "gy"),
            P(None, None, None, "gx", "gy"),
            P(),
            P(),
            P("gx", "gy"),
        ),
        out_specs=(P(None, "gx", "gy"), P("gx", "gy")),
        check_vma=False,
    )
```

```python
import functools

import jax
import jax.numpy as jnp
import numpy as np
from jax import lax
from jax.experimental import pallas as pl
from jax.experimental.pallas import tpu as pltpu
from jax.sharding import PartitionSpec as P

STEPS = 24
NF = 3
RADIUS = 3
COURANT = 0.68

T = 256
PAD = 32
ROWS = T + 2 * PAD
CHUNK = ROWS // 8
HALF = CHUNK // 2
LANES = 128
UNROLL = 6
PLANES = 6 * NF
K = 8 * 2 * NF

f32 = jnp.float32
bf16 = jnp.bfloat16


def filter_table():
    offsets = np.arange(-RADIUS, RADIUS + 1)
    dist = np.sqrt(offsets[:, None] ** 2 + offsets[None, :] ** 2)
    table = np.maximum(0.0, RADIUS - dist)
    return table / table.sum()


def lane_iota():
    return lax.broadcasted_iota(jnp.int32, (8, LANES), 1)


def turn(x, shift, axis):
    size = x.shape[axis]
    shift = shift % size
    return x if shift == 0 else pltpu.roll(x, shift, axis)


def right_slot(group, k):
    return 32 * ((group + (2 if k >= 4 else 0)) % 4)


def left_slot(group, k):
    return 32 * ((group + (3 if k >= 4 else 1)) % 4)


def chunked(body, times):
    def several(i, _):
        for u in range(times):
            body(times * i + u)
        return 0

    lax.fori_loop(0, HALF // times, several, 0)


def riders(k):
    return [(jj, m) for jj, m in enumerate(range(3 * k, 3 * k + 3)) if m <= PLANES]


def x_slab(side, plane, rider, write):
    sub = lax.broadcasted_iota(jnp.int32, (8, T), 0)
    for k in range(7):
        edge = plane(k, 0 if side == 0 else 24)
        for jj, m in riders(k):
            edge = jnp.where(sub // 2 == jj + side, turn(rider(m), 2 * jj + 2, 0), edge)
        for j in range(4):
            write(k, 8 * j, edge if j == 3 * side else plane(k, 8 * j))


def pack_kernel(fields, inv_eps, fwd, mask, xs0, xs1, ys0, ys1, f7, fw, mk, sems):
    even_x = lax.rem(lax.axis_index("gx"), 2) == 0
    even_y = lax.rem(lax.axis_index("gy"), 2) == 0
    loads = [[
        pltpu.make_async_copy(inv_eps, f7.at[6], sems.at[0]),
        pltpu.make_async_copy(mask, mk, sems.at[1]),
    ]]
    for k in range(6):
        loads.append([
            pltpu.make_async_copy(fields.at[k], f7.at[k], sems.at[2 + k]),
            pltpu.make_async_copy(fwd.at[pl.ds(3 * k, 3)], fw.at[pl.ds(3 * k, 3)], sems.at[8 + k]),
        ])
    for piece in loads:
        for copy in piece:
            copy.start()
    lane = lane_iota()

    def rows(ref, k, g, j, t):
        return ref[k, pl.ds(64 * g + 8 * j, 8), pl.ds(LANES * t, LANES)]

    for k, piece in zip((6, 0, 1, 2, 3, 4, 5), loads, strict=True):
        for copy in piece:
            copy.wait()
        if k == 6:
            fw[PLANES] = mk[...].astype(f32)
        for j in range(8):
            first = last = None
            for g in range(4):
                a = turn(rows(f7, k, g, j, 0), right_slot(g, k), 1)
                b = turn(rows(f7, k, g, j, 1), left_slot(g, k) - 96, 1)
                first = a if g == 0 else jnp.where(lane // 32 == right_slot(g, k) // 32, a, first)
                last = b if g == 0 else jnp.where(lane // 32 == left_slot(g, k) // 32, b, last)
            for jj, m in riders(k):
                for g in range(4):
                    a, b = right_slot(g, k) + 26 + 2 * jj, left_slot(g, k) + 2 * jj
                    first = jnp.where(lane // 2 == a // 2, turn(rows(fw, m, g, j, 0), a, 1), first)
                    last = jnp.where(lane // 2 == b // 2, turn(rows(fw, m, g, j, 1), b - 126, 1), last)
            to = pl.ds(8 * j, 8)
            ys0[k, to] = jnp.where(even_y, last, first)
            ys1[k, to] = jnp.where(even_y, first, last)

    def write(side):
        def put_row(k, row, value):
            if side == 0:
                xs0[k, pl.ds(row, 8)] = value
            else:
                xs1[k, pl.ds(row, 8)] = value

        return put_row

    for flip, here in ((0, even_x), (1, jnp.logical_not(even_x))):
        @pl.when(here)
        def _():
            for side, (base, near) in enumerate(((T - 32, T - 8), (0, 0))):
                x_slab(
                    side,
                    lambda k, row: f7[k, pl.ds(base + row, 8)],
                    lambda m: fw[m, pl.ds(near, 8)],
                    write(side ^ flip),
                )


def pack(fields, inv_eps, fwd, mask):
    x_shape = jax.ShapeDtypeStruct((7, 32, T), f32)
    y_shape = jax.ShapeDtypeStruct((7, 64, LANES), f32)
    return pl.pallas_call(
        pack_kernel,
        out_shape=(x_shape, x_shape, y_shape, y_shape),
        in_specs=[pl.BlockSpec(memory_space=pl.ANY)] * 4,
        out_specs=(pl.BlockSpec(memory_space=pltpu.VMEM),) * 4,
        scratch_shapes=[
            pltpu.VMEM((7, T, T), f32),
            pltpu.VMEM((PLANES + 1, T, T), f32),
            pltpu.VMEM((T, T), jnp.int32),
            pltpu.SemaphoreType.DMA((14,)),
        ],
        compiler_params=pltpu.CompilerParams(vmem_limit_bytes=56 * 2**20),
        cost_estimate=pl.CostEstimate(flops=10**7, bytes_accessed=7 * 10**6, transcendentals=0),
        name="pack",
    )(fields, inv_eps, fwd, mask)


def half_turn(x):
    return turn(x, LANES // 2, 1)


def next_lane(q, lane, by=1):
    a0, a1, b0, b1, x = [turn(z, -by, 1) for z in q]
    end, mid = lane >= LANES - by, (lane >= 64 - by) & (lane < 64)
    return [
        jnp.where(end, a1, a0),
        jnp.where(end, x, a1),
        jnp.where(mid, b1, b0),
        jnp.where(mid, x, b1),
        jnp.where(end, a0, jnp.where(mid, b0, x)),
    ]


def prev_lane(q, lane, by=1):
    a0, a1, b0, b1, x = [turn(z, by, 1) for z in q]
    end, mid = lane < by, (lane >= 64) & (lane < 64 + by)
    return [
        jnp.where(end, x, a0),
        jnp.where(end, a0, a1),
        jnp.where(mid, x, b0),
        jnp.where(mid, b0, b1),
        jnp.where(end, a1, jnp.where(mid, b1, x)),
    ]


def of_first(lane):
    return (lane < 32) | (lane >= 96)


def wrap_next(q, lane):
    a0, a1, b0, b1, x = [half_turn(z) for z in q]
    return [b0, b1, turn(a0, -1, 0), turn(a1, -1, 0), jnp.where(of_first(lane), x, turn(x, -1, 0))]


def wrap_prev(q, lane):
    a0, a1, b0, b1, x = [half_turn(z) for z in q]
    return [turn(b0, 1, 0), turn(b1, 1, 0), a0, a1, jnp.where(of_first(lane), turn(x, 1, 0), x)]


def load_pair(plane, u, lane):
    v, w = pl.ds(u, 8, stride=CHUNK), pl.ds(u + HALF, 8, stride=CHUNK)
    res = [plane(t)[v, :] for t in range(2)] + [half_turn(plane(t)[w, :]) for t in range(2)]
    return res + [jnp.where(of_first(lane), plane(2)[v, :], half_turn(plane(2)[w, :]))]


def store_pair(plane, u, q):
    v, w = pl.ds(u, 8, stride=CHUNK), pl.ds(u + HALF, 8, stride=CHUNK)
    for t in range(2):
        plane(t)[v, :] = q[t]
        plane(t)[w, :] = half_turn(q[2 + t])


def main_kernel(table, fields, inv_eps, fwd, mask, y0, y1, x0, x1, c0, c1, out, grad,
                stage, fst, mk, yl, yr, cl, ch, coef, e, h, fac, raw, sems):
    px = lax.rem(lax.axis_index("gx"), 2)
    py = lax.rem(lax.axis_index("gy"), 2)
    own = pl.ds(PAD, T)
    copies, late = [], []
    for t in range(2):
        cols = pl.ds(LANES * t, LANES)
        copies.append(pltpu.make_async_copy(fields.at[:, :, cols], stage.at[pl.ds(0, 6), t, own], sems.at[t]))
        copies.append(pltpu.make_async_copy(inv_eps.at[:, cols], stage.at[6, t, own], sems.at[2 + t]))
        late.append(pltpu.make_async_copy(fwd.at[:, :, cols], fst.at[pl.ds(0, PLANES), t, own], sems.at[4 + t]))
    late.append(pltpu.make_async_copy(mask, mk, sems.at[6]))

    def edges(low, high, left, right, clow, chigh):
        res = []
        for t in range(2):
            cols = pl.ds(LANES * t, LANES)
            res.append(pltpu.make_async_copy(low.at[:, :, cols], stage.at[:, t, pl.ds(0, PAD)], sems.at[7 + t]))
            res.append(pltpu.make_async_copy(high.at[:, :, cols], stage.at[:, t, pl.ds(PAD + T, PAD)], sems.at[9 + t]))
        res.append(pltpu.make_async_copy(left, yl, sems.at[11]))
        res.append(pltpu.make_async_copy(right, yr, sems.at[12]))
        res.append(pltpu.make_async_copy(clow, cl, sems.at[13]))
        res.append(pltpu.make_async_copy(chigh, ch, sems.at[14]))
        return res

    for ix in range(2):
        for iy in range(2):
            @pl.when((px == ix) & (py == iy))
            def _():
                xs = (x1, x0) if ix == 0 else (x0, x1)
                ys = (y1, y0) if iy == 0 else (y0, y1)
                cs = (c1, c0) if ix == 0 else (c0, c1)
                for copy in edges(*xs, *ys, *cs):
                    copy.start()
    for copy in copies + late:
        copy.start()

    row = lax.broadcasted_iota(jnp.int32, (16, 3 * K), 0)
    col = lax.broadcasted_iota(jnp.int32, (16, 3 * K), 1)

    def spread(i, _):
        block = jnp.zeros((16, 3 * K), f32)
        for u in range(2):
            for j in range(6 * NF):
                block = jnp.where((row == col - 8 * j + 8 * u) & (col // 8 == j), table[2 * i + u, j], block)
        coef[pl.ds(pl.multiple_of(16 * i, 16), 16)] = block.astype(bf16)
        return 0

    lax.fori_loop(0, STEPS // 2, spread, 0)

    for copy in edges(x0, x1, y0, y1, c0, c1):
        copy.wait()

    lane = lane_iota()
    sub = lax.broadcasted_iota(jnp.int32, (8, LANES), 0)
    right_half = lane < 64

    def fill(j):
        at = pl.ds(8 * j, 8)
        for k in range(7):
            r, l = yr[k, at], yl[k, at]
            for g in range(4):
                to = pl.ds(PAD + 64 * g + 8 * j, 8)
                stage[k, 2, to] = jnp.where(
                    right_half, turn(r, -right_slot(g, k), 1), turn(l, 96 - left_slot(g, k), 1)
                )
                for jj, m in enumerate(range(3 * k, min(3 * k + 3, PLANES + 1))):
                    fst[m, 2, to] = jnp.where(
                        right_half,
                        turn(r, -right_slot(g, k) - 26 - 2 * jj, 1),
                        turn(l, 126 - left_slot(g, k) - 2 * jj, 1),
                    )

    for j in range(8):
        fill(j)
    zero = jnp.zeros((8, LANES), f32)
    for k in range(7):
        c = k % 4
        rl, ll, rh, lh = right_slot(3, k), left_slot(3, k), right_slot(0, k), left_slot(0, k)
        for j in range(4):
            a, b = cl[c, pl.ds(8 * j, 8)], ch[c, pl.ds(8 * j, 8)]
            stage[k, 2, pl.ds(8 * j, 8)] = jnp.where(right_half, turn(a, -rl, 1), turn(a, 96 - ll, 1))
            stage[k, 2, pl.ds(PAD + T + 8 * j, 8)] = jnp.where(right_half, turn(b, -rh, 1), turn(b, 96 - lh, 1))
        a, b = cl[c, pl.ds(24, 8)], ch[c, pl.ds(0, 8)]
        for jj, m in riders(k):
            fst[m, 2, pl.ds(24, 8)] = jnp.where(
                right_half, turn(a, -rl - 26 - 2 * jj, 1), turn(a, 126 - ll - 2 * jj, 1)
            )
            fst[m, 2, pl.ds(PAD + T, 8)] = jnp.where(
                right_half, turn(b, -rh - 26 - 2 * jj, 1), turn(b, 126 - lh - 2 * jj, 1)
            )
            for t in range(2):
                lo, hi = stage[k, t, pl.ds(0, 8)], stage[k, t, pl.ds(ROWS - 8, 8)]
                fst[m, t, pl.ds(24, 8)] = jnp.where(sub >= 6, turn(lo, 6 - 2 * jj, 0), 0.0)
                fst[m, t, pl.ds(PAD + T, 8)] = jnp.where(sub < 2, turn(hi, -2 - 2 * jj, 0), 0.0)
            for t in range(3):
                for j in range(3):
                    fst[m, t, pl.ds(8 * j, 8)] = zero
                    fst[m, t, pl.ds(PAD + T + 8 + 8 * j, 8)] = zero

    def staged(ref, k):
        return lambda t: ref.at[k, t]

    def put(ref, q, u):
        for i in range(5):
            ref[u, i] = q[i]

    def get(ref, u):
        return [ref[u, i] for i in range(5)]

    def lift(u):
        for c in range(3):
            put(e.at[0, c], load_pair(staged(stage, c), u, lane), u)
            put(h.at[c], [z * (1.0 / COURANT) for z in load_pair(staged(stage, 3 + c), u, lane)], u)
        put(fac, [z * (COURANT * COURANT) for z in load_pair(staged(stage, 6), u, lane)], u)

    for copy in copies:
        copy.wait()
    chunked(lift, 10)

    def step(n, first):
        old, new = e.at[n], e.at[n + 1]

        def after(c, u):
            return get(old.at[c], u + 1) if u < HALF - 1 else wrap_next(get(old.at[c], 0), lane)

        ey, ez = get(old.at[1], first), get(old.at[2], first)
        for k in range(HALF):
            u = (first + k) % HALF
            if u == 0 and k > 0:
                ey, ez = get(old.at[1], 0), get(old.at[2], 0)
            ex, ey_n, ez_n = get(old.at[0], u), after(1, u), after(2, u)
            xn, zn = next_lane(ex, lane), next_lane(ez, lane)
            hx, hy, hz = get(h.at[0], u), get(h.at[1], u), get(h.at[2], u)
            for i in range(5):
                hx[i] = hx[i] - (zn[i] - ez[i])
                hy[i] = hy[i] + (ez_n[i] - ez[i])
                hz[i] = hz[i] - ((ey_n[i] - ey[i]) - (xn[i] - ex[i]))
            put(h.at[0], hx, u)
            put(h.at[1], hy, u)
            put(h.at[2], hz, u)
            ey, ez = ey_n, ez_n
        hy_p, hz_p = get(h.at[1], first), get(h.at[2], first)
        for k in range(HALF):
            u = (first + 1 + k) % HALF
            if u == 0:
                hy_p, hz_p = wrap_prev(hy_p, lane), wrap_prev(hz_p, lane)
            hx, hy, hz = get(h.at[0], u), get(h.at[1], u), get(h.at[2], u)
            xp, zp, f = prev_lane(hx, lane), prev_lane(hz, lane), get(fac, u)
            ex, ey, ez = get(old.at[0], u), get(old.at[1], u), get(old.at[2], u)
            for i in range(5):
                ex[i] = ex[i] + f[i] * (hz[i] - zp[i])
                ey[i] = ey[i] - f[i] * (hz[i] - hz_p[i])
                ez[i] = ez[i] + f[i] * ((hy[i] - hy_p[i]) - (hx[i] - xp[i]))
            put(new.at[0], ex, u)
            put(new.at[1], ey, u)
            put(new.at[2], ez, u)
            hy_p, hz_p = hy, hz

    def steps(i, _):
        for k in range(UNROLL):
            step(UNROLL * i + k, k)
        return 0

    lax.fori_loop(0, STEPS // UNROLL, steps, 0)

    for copy in late:
        copy.wait()
    for t in range(2):
        fst[PLANES, t, own] = mk[:, pl.ds(LANES * t, LANES)].astype(f32)

    def lower(u):
        for c in range(3):
            store_pair(staged(stage, c), u, get(e.at[STEPS, c], u))
            store_pair(staged(stage, 3 + c), u, [z * COURANT for z in get(h.at[c], u)])

    chunked(lower, 10)
    stores = [
        pltpu.make_async_copy(stage.at[pl.ds(0, 6), t, own], out.at[:, :, pl.ds(LANES * t, LANES)], sems.at[t])
        for t in range(2)
    ]
    for copy in stores:
        copy.start()

    def gather(u):
        total = [zero] * 5
        for c in range(3):
            w = jnp.concatenate(
                [jnp.concatenate(load_pair(staged(fst, 3 * i + c), u, lane), axis=1) for i in range(2 * NF)], axis=0
            )
            hi = w.astype(bf16)
            lo = (w - hi.astype(f32)).astype(bf16)
            g = jnp.dot(coef[...], jnp.concatenate([hi, hi, lo], axis=0), preferred_element_type=f32)
            for n in range(STEPS):
                for i in range(5):
                    total[i] = total[i] + e[n + 1, c, u, i] * g[8 * n : 8 * n + 8, LANES * i : LANES * i + LANES]
        part = load_pair(staged(fst, PLANES), u, lane)
        put(raw, [total[i] * part[i] for i in range(5)], u + 2)

    chunked(gather, 10)
    for i in range(2):
        put(raw, wrap_prev(get(raw, HALF + i), lane), i)
        put(raw, wrap_next(get(raw, 2 + i), lane), HALF + 2 + i)

    taps = filter_table()

    def smooth(u):
        part = [[], [], []]
        for i in range(5):
            r0 = raw[u + 2, i]
            r1 = raw[u + 1, i] + raw[u + 3, i]
            r2 = raw[u, i] + raw[u + 4, i]
            for b in range(3):
                part[b].append(float(taps[3, 3 + b]) * r0 + float(taps[4, 3 + b]) * r1 + float(taps[5, 3 + b]) * r2)
        acc = part[0]
        for b in (1, 2):
            up, down = next_lane(part[b], lane, b), prev_lane(part[b], lane, b)
            acc = [acc[i] + (up[i] + down[i]) for i in range(4)]
        store_pair(staged(stage, 6), u, acc)

    chunked(smooth, 10)
    stores += [
        pltpu.make_async_copy(stage.at[6, t, own], grad.at[:, pl.ds(LANES * t, LANES)], sems.at[2 + t]) for t in range(2)
    ]
    for copy in stores[2:]:
        copy.start()
    for copy in stores:
        copy.wait()


def advance(table, fields, inv_eps, fwd, mask, *edges):
    any_space = pl.BlockSpec(memory_space=pl.ANY)
    return pl.pallas_call(
        main_kernel,
        out_shape=(jax.ShapeDtypeStruct((6, T, T), f32), jax.ShapeDtypeStruct((T, T), f32)),
        in_specs=[pl.BlockSpec(memory_space=pltpu.SMEM)] + [any_space] * 10,
        out_specs=(any_space,) * 2,
        scratch_shapes=[
            pltpu.VMEM((7, 3, ROWS, LANES), f32),
            pltpu.VMEM((PLANES + 1, 3, ROWS, LANES), f32),
            pltpu.VMEM((T, T), jnp.int32),
            pltpu.VMEM((7, 64, LANES), f32),
            pltpu.VMEM((7, 64, LANES), f32),
            pltpu.VMEM((4, 32, LANES), f32),
            pltpu.VMEM((4, 32, LANES), f32),
            pltpu.VMEM((2 * STEPS * 4, 3 * K), bf16),
            pltpu.VMEM((STEPS + 1, 3, HALF, 5, 8, LANES), f32),
            pltpu.VMEM((3, HALF, 5, 8, LANES), f32),
            pltpu.VMEM((HALF, 5, 8, LANES), f32),
            pltpu.VMEM((HALF + 4, 5, 8, LANES), f32),
            pltpu.SemaphoreType.DMA((15,)),
        ],
        compiler_params=pltpu.CompilerParams(vmem_limit_bytes=48 * 2**20),
        name="advance",
    )(table, fields, inv_eps, fwd, mask, *edges)


def swap(x, axis, offset):
    count = lax.axis_size(axis)
    route = []
    for i in range(offset, count + offset, 2):
        a, b = i % count, (i + 1) % count
        route += [(a, b), (b, a)]
    return lax.ppermute(x, axis, route)


def coefficients(phase_start, omega):
    theta = phase_start[None] + omega[None] * jnp.arange(STEPS, dtype=f32)[:, None]
    table = jnp.stack([jnp.cos(theta), -jnp.sin(theta)], axis=2).reshape(STEPS, 2 * NF) / STEPS
    high = lax.reduce_precision(table, 8, 7)
    low = lax.reduce_precision(table - high, 8, 7)
    return jnp.concatenate([high, low, high], axis=1)


def local(fields, inv_eps, fwd_dft, phase_start, omega, mask):
    fwd = fwd_dft.reshape(PLANES, T, T)
    table = coefficients(phase_start, omega)
    xs0, xs1, ys0, ys1 = pack(fields, inv_eps, fwd, mask)
    y0 = swap(ys0, "gy", 0)
    y1 = swap(ys1, "gy", 1)
    x0 = swap(xs0, "gx", 0)
    x1 = swap(xs1, "gx", 1)
    even_x = lax.rem(lax.axis_index("gx"), 2) == 0
    even_y = lax.rem(lax.axis_index("gy"), 2) == 0
    right = jnp.where(even_y, y0, y1)
    left = jnp.where(even_y, y1, y0)
    lane = lax.broadcasted_iota(jnp.int32, (4, 32, LANES), 2)

    def corner(rows, group):
        r, l = right[:, rows], left[:, rows]
        r4, l4 = jnp.concatenate([r[4:], r[:1]]), jnp.concatenate([l[4:], l[:1]])
        block = lane // 32 * 32
        res = jnp.where(block == right_slot(group, 0), r[:4], l[:4])
        res = jnp.where(block == right_slot(group, 4), r4, res)
        return jnp.where(block == left_slot(group, 4), l4, res)

    up, down = corner(slice(32, 64), 3), corner(slice(0, 32), 0)
    c0 = swap(jnp.where(even_x, up, down), "gx", 0)
    c1 = swap(jnp.where(even_x, down, up), "gx", 1)
    return advance(table, fields, inv_eps, fwd, mask, y0, y1, x0, x1, c0, c1)


def solution(mesh):
    return jax.shard_map(
        local,
        mesh=mesh,
        in_specs=(
            P(None, "gx", "gy"),
            P("gx", "gy"),
            P(None, None, None, "gx", "gy"),
            P(),
            P(),
            P("gx", "gy"),
        ),
        out_specs=(P(None, "gx", "gy"), P("gx", "gy")),
        check_vma=False,
    )
```
